32 devices in a mesh: blk: 32 (over z, y, x, core).
Axes of the slice: x: 2, y: 2, z: 4, core: 2. Of those that a mesh axis runs over, the one named last changes fastest.
Arguments:
- blocks: float32 [4, 512, 256, 128], P(None, 'blk'), may hold values from -6 to 6
- first: float32 [512, 256], P('blk'), may hold values from -2.4 to 2.4
- second: float32 [8192, 256], P('blk'), may hold values from -2.4 to 2.4
- third: float32 [4096, 256], P('blk'), may hold values from -2.4 to 2.4
Outputs:
- first_final: float32 [512, 256], P('blk')
- second_final: float32 [8192, 256], P('blk')
- third_final: float32 [4096, 256], P('blk')
The draws below stay inside these ranges and needn't reach their ends.
All inputs are finite; a program needn't handle non-finite values.
Results may differ from the reference program's by a relative error of at most 0.0003.
Values sent between devices are 32-bit elements; how exact they have to be, the bound alone decides.
A program may use at most 64 MiB of HBM per device.

```python
import jax
import jax.numpy as jnp
from jax import lax

RANK = 256
STRATA = 4
I_DEV = 16
J_DEV = 256
K_DEV = 128
BLOCKS = 32
I_ROWS = 512
J_ROWS = 8192
K_ROWS = 4096


def levels(stream_key, dims, shards, smallest, top_value):
    gain = 1.0
    for dim, blocks in shards:
        steps = jax.random.uniform(jax.random.fold_in(jax.random.fold_in(stream_key, 6), dim), (blocks,), jnp.float32, smallest / len(shards), top_value / len(shards))
        gain = gain * jnp.repeat(jnp.exp(steps), dims[dim] // blocks).reshape((-1,) + (1,) * (len(dims) - 1 - dim))
    return gain


def noise(key, dims, scale, most, cuts=(), kind=jnp.bfloat16):
    result = scale * jax.random.normal(key, dims, jnp.float32)
    if cuts:
        result = result * levels(key, dims, cuts, -0.22, 0.18)
    return jnp.clip(result, -most, most).astype(kind)


def setup_inputs(seed: int = 0) -> dict:
    key_list = jax.random.split(jax.random.key(seed), 5)
    return {
        "blocks": noise(key_list[0], (STRATA, I_ROWS, J_DEV, K_DEV), 1.0, 6.0, ((1, 32),), jnp.float32),
        "first": noise(key_list[1], (I_ROWS, RANK), 0.4, 2.4, ((0, 32),), jnp.float32),
        "second": noise(key_list[2], (J_ROWS, RANK), 0.4, 2.4, ((0, 32),), jnp.float32),
        "third": noise(key_list[3], (K_ROWS, RANK), 0.4, 2.4, ((0, 32),), jnp.float32),
    }


momentum = 0.5
step_scale = 8.0


def gradients(target, first_block, second_block, third_block):
    first_rows = first_block.shape[0]
    second_rows = second_block.shape[0]
    paired = (first_block[:, None, :] * second_block[None, :, :]).reshape(first_rows * second_rows, -1)
    modeled = jnp.dot(paired, third_block.T, precision=lax.Precision.HIGHEST)
    misfit = modeled - target.reshape(first_rows * second_rows, -1)
    contracted = jnp.dot(misfit, third_block, precision=lax.Precision.HIGHEST).reshape(first_rows, second_rows, -1)
    grad_first = jnp.sum(contracted * second_block[None, :, :], axis=1)
    grad_second = jnp.sum(contracted * first_block[:, None, :], axis=0)
    grad_third = lax.dot_general(misfit, paired, (((0,), (0,)), ((), ())), precision=lax.Precision.HIGHEST)
    return grad_first, grad_second, grad_third


def advance(factor, velocity, gradient, rate):
    keep = momentum * velocity
    step = rate * gradient
    return (factor + keep) - step, keep - step


def device_grads(parts):
    return gradients(parts[0], parts[1], parts[2], parts[3])


def reference(blocks, first, second, third):
    first_blk = first.reshape(BLOCKS, I_DEV, RANK)
    second_blk = second.reshape(BLOCKS, J_DEV, RANK)
    third_blk = third.reshape(BLOCKS, K_DEV, RANK)
    vel_first = jnp.zeros_like(first_blk)
    vel_second = jnp.zeros_like(second_blk)
    vel_third = jnp.zeros_like(third_blk)
    rate_first = step_scale / (J_DEV * K_DEV)
    rate_second = step_scale / (I_DEV * K_DEV)
    rate_third = step_scale / (I_DEV * J_DEV)
    for stratum in range(STRATA):
        second_now = jnp.roll(second_blk, -stratum, axis=0)
        third_now = jnp.roll(third_blk, -3 * stratum, axis=0)
        target = blocks[stratum].reshape(BLOCKS, I_DEV, J_DEV, K_DEV)
        grad_first, grad_second, grad_third = lax.map(device_grads, (target, first_blk, second_now, third_now))
        grad_second = jnp.roll(grad_second, stratum, axis=0)
        grad_third = jnp.roll(grad_third, 3 * stratum, axis=0)
        first_blk, vel_first = advance(first_blk, vel_first, grad_first, rate_first)
        second_blk, vel_second = advance(second_blk, vel_second, grad_second, rate_second)
        third_blk, vel_third = advance(third_blk, vel_third, grad_third, rate_third)
    return (first_blk.reshape(I_ROWS, RANK), second_blk.reshape(J_ROWS, RANK), third_blk.reshape(K_ROWS, RANK))
```

```python
import functools

import jax
import jax.numpy as jnp
from jax import lax
from jax.experimental import pallas as pl
from jax.experimental.pallas import tpu as pltpu
from jax.sharding import PartitionSpec as P

momentum = 0.5
step_scale = 8.0
third_stride = 3
MESH = pl.DeviceIdType.MESH
NT = (((1,), (1,)), ((), ()))


def halves(x):
    high = x.astype(jnp.bfloat16)
    low = (x - high.astype(jnp.float32)).astype(jnp.bfloat16)
    return high, low


def dot(a, b):
    return jnp.dot(a, b, preferred_element_type=jnp.float32)


def kernel(
    count, strata, rates,
    blocks, first, second, third,
    first_out, second_out, third_out,
    target, rows_a, vel_a, grad_a, grad_c,
    recv_b, recv_c, send_b, send_c, past_b, past_c,
    keep_out_b, keep_out_c, keep_in_b, keep_in_c, last_b, last_c,
    cat_k, cat_r, pair_h, pair_l, miss, turn_h, turn_l,
    t_sem, b_sem, c_sem, pb_sem, pc_sem, kb_sem, kc_sem, lb_sem, lc_sem,
):
    rate_a, rate_b, rate_c = rates
    me = lax.axis_index("blk")
    i_rows = first.shape[0]
    j_rows, rank = second.shape
    k_rows = third.shape[0]
    wide = 2 * k_rows

    def other(by):
        return lax.rem(me + (by % count), count)

    def to(src, dst, sem, by):
        return pltpu.make_async_remote_copy(
            src_ref=src, dst_ref=dst, send_sem=sem.at[0], recv_sem=sem.at[1],
            device_id=(other(by),), device_id_type=MESH,
        )

    hops = set()
    for reach in (1, strata - 2, strata - 1):
        hops |= {reach, -reach, third_stride * reach, -third_stride * reach}
    hops = sorted(hops)
    barrier = pltpu.get_barrier_semaphore()
    for by in hops:
        pl.semaphore_signal(barrier, inc=1, device_id=(other(by),), device_id_type=MESH)
    loads = [
        pltpu.make_async_copy(blocks.at[s], target.at[s], t_sem.at[s]) for s in range(strata)
    ]
    for load in loads:
        load.start()
    pl.semaphore_wait(barrier, len(hops))

    rows_a[...] = first[...]
    sent = []
    for s in range(strata):
        if s == 0:
            b_ref, c_ref = second, third
        else:
            b_ref, c_ref = recv_b.at[s - 1], recv_c.at[s - 1]
            moved_c.wait_recv()
            moved_b.wait_recv()
        if s + 2 < strata:
            past = (
                to(c_ref, past_c.at[s], pc_sem.at[s], -third_stride),
                to(b_ref, past_b.at[s], pb_sem.at[s], -1),
            )
            for copy in past:
                copy.start()
            sent.extend(past)
        b_high, b_low = halves(b_ref[...])
        cat_k[...] = jnp.concatenate([b_high, b_high, b_low], axis=1)
        cat_r[...] = jnp.concatenate([b_high, b_high, b_low], axis=0)
        loads[s].wait()

        def model(p, _):
            c = c_ref[...]
            a0 = rows_a[pl.ds(2 * p, 1), :]
            a1 = rows_a[pl.ds(2 * p + 1, 1), :]
            high, low = halves(jnp.concatenate([c * a0, c * a1], axis=0))
            at = pl.multiple_of(p * wide, wide)
            pair_h[pl.ds(at, wide), :] = high
            pair_l[pl.ds(at, wide), :] = low
            made = lax.dot_general(
                cat_k[...], jnp.concatenate([high, low, high], axis=1), NT,
                preferred_element_type=jnp.float32,
            )
            want = jnp.concatenate([target[s, 2 * p], target[s, 2 * p + 1]], axis=1)
            high, low = halves(made - want)
            miss[pl.ds(0, j_rows), pl.ds(at, wide)] = high
            miss[pl.ds(j_rows, j_rows), pl.ds(at, wide)] = low
            turn_h[pl.ds(at, wide), :] = high.T
            turn_l[pl.ds(at, wide), :] = low.T
            return 0

        lax.fori_loop(0, i_rows // 2, model, 0, unroll=2)

        both = dot(miss[...], pair_h[...])
        grad = both[:j_rows] + both[j_rows:] + dot(miss[pl.ds(0, j_rows), :], pair_l[...])
        step_b = rate_b * grad
        if s + 1 == strata:
            send_b[s] = step_b
            moved_b = to(send_b.at[s], last_b, lb_sem, strata - 1)
            moved_b.start()
        else:
            now = b_ref[...]
            if s > 0:
                old_b.wait_recv()
                keep = momentum * (now - past_b[s - 1])
                now = now + keep
                vel = keep - step_b
            else:
                vel = -step_b
            now = now - step_b
            send_b[s] = now
            moved_b = to(send_b.at[s], recv_b.at[s], b_sem.at[s], -1)
            moved_b.start()
            if s + 2 == strata:
                keep_out_b[...] = now + momentum * vel
        sent.append(moved_b)

        grad_c[...] = jnp.zeros_like(grad_c)

        def spread(p, _):
            at = pl.multiple_of(p * wide, wide)
            high = turn_h[pl.ds(at, wide), :]
            low = turn_l[pl.ds(at, wide), :]
            d = dot(jnp.concatenate([high, low, high], axis=1), cat_r[...])
            c = c_ref[...]
            a0 = rows_a[pl.ds(2 * p, 1), :]
            a1 = rows_a[pl.ds(2 * p + 1, 1), :]
            grad_c[...] += a0 * d[:k_rows] + a1 * d[k_rows:]
            grad_a[pl.ds(2 * p, 1), :] = jnp.sum(c * d[:k_rows], axis=0, keepdims=True)
            grad_a[pl.ds(2 * p + 1, 1), :] = jnp.sum(c * d[k_rows:], axis=0, keepdims=True)
            return 0

        lax.fori_loop(0, i_rows // 2, spread, 0, unroll=2)

        step_c = rate_c * grad_c[...]
        if s + 1 == strata:
            send_c[s] = step_c
            moved_c = to(send_c.at[s], last_c, lc_sem, third_stride * (strata - 1))
            moved_c.start()
        else:
            now = c_ref[...]
            if s > 0:
                old_c.wait_recv()
                keep = momentum * (now - past_c[s - 1])
                now = now + keep
                vel = keep - step_c
            else:
                vel = -step_c
            now = now - step_c
            send_c[s] = now
            moved_c = to(send_c.at[s], recv_c.at[s], c_sem.at[s], -third_stride)
            moved_c.start()
            if s + 2 == strata:
                keep_out_c[...] = now + momentum * vel
                kept_b = to(keep_out_b, keep_in_b, kb_sem, strata - 2)
                kept_c = to(keep_out_c, keep_in_c, kc_sem, third_stride * (strata - 2))
                kept_b.start()
                kept_c.start()
                sent.extend([kept_b, kept_c])
        sent.append(moved_c)
        if s + 2 < strata:
            old_c, old_b = past

        step_a = rate_a * grad_a[...]
        if s == 0:
            rows_a[...] = rows_a[...] - step_a
            vel_a[...] = -step_a
        else:
            keep = momentum * vel_a[...]
            rows_a[...] = (rows_a[...] + keep) - step_a
            vel_a[...] = keep - step_a

    first_out[...] = rows_a[...]
    kept_b.wait_recv()
    moved_b.wait_recv()
    second_out[...] = keep_in_b[...] - last_b[...]
    kept_c.wait_recv()
    moved_c.wait_recv()
    third_out[...] = keep_in_c[...] - last_c[...]
    for copy in sent:
        copy.wait_send()


def shards(count, blocks, first, second, third):
    strata = blocks.shape[0]
    i_rows, rank = first.shape
    j_rows = second.shape[0]
    k_rows = third.shape[0]
    rates = (
        step_scale / (j_rows * k_rows),
        step_scale / (i_rows * k_rows),
        step_scale / (i_rows * j_rows),
    )
    f32, bf16 = jnp.float32, jnp.bfloat16
    a, b, c = (i_rows, rank), (j_rows, rank), (k_rows, rank)
    pairs = i_rows * k_rows
    vmem = pl.BlockSpec(memory_space=pltpu.VMEM)
    dma = pltpu.SemaphoreType.DMA
    return pl.pallas_call(
        functools.partial(kernel, count, strata, rates),
        out_shape=[jax.ShapeDtypeStruct(x, f32) for x in (a, b, c)],
        in_specs=[pl.BlockSpec(memory_space=pl.ANY), vmem, vmem, vmem],
        out_specs=[vmem, vmem, vmem],
        scratch_shapes=[
            pltpu.VMEM(blocks.shape, f32),
            pltpu.VMEM(a, f32), pltpu.VMEM(a, f32), pltpu.VMEM(a, f32), pltpu.VMEM(c, f32),
            pltpu.VMEM((strata - 1,) + b, f32), pltpu.VMEM((strata - 1,) + c, f32),
            pltpu.VMEM((strata,) + b, f32), pltpu.VMEM((strata,) + c, f32),
            pltpu.VMEM((strata - 2,) + b, f32), pltpu.VMEM((strata - 2,) + c, f32),
            pltpu.VMEM(b, f32), pltpu.VMEM(c, f32),
            pltpu.VMEM(b, f32), pltpu.VMEM(c, f32),
            pltpu.VMEM(b, f32), pltpu.VMEM(c, f32),
            pltpu.VMEM((j_rows, 3 * rank), bf16), pltpu.VMEM((3 * j_rows, rank), bf16),
            pltpu.VMEM((pairs, rank), bf16), pltpu.VMEM((pairs, rank), bf16),
            pltpu.VMEM((2 * j_rows, pairs), bf16),
            pltpu.VMEM((pairs, j_rows), bf16), pltpu.VMEM((pairs, j_rows), bf16),
            dma((strata,)),
            dma((strata - 1, 2)), dma((strata - 1, 2)),
            dma((strata - 2, 2)), dma((strata - 2, 2)),
            dma((2,)), dma((2,)), dma((2,)), dma((2,)),
        ],
        compiler_params=pltpu.CompilerParams(
            collective_id=0, has_side_effects=True, vmem_limit_bytes=48 * 1024 * 1024,
        ),
        cost_estimate=pl.CostEstimate(
            flops=strata * 18 * pairs * j_rows * rank,
            bytes_accessed=4 * strata * i_rows * j_rows * k_rows, transcendentals=0,
        ),
    )(blocks, first, second, third)


def solution(mesh):
    return jax.shard_map(
        functools.partial(shards, mesh.shape["blk"]),
        mesh=mesh,
        in_specs=(P(None, "blk", None, None), P("blk", None), P("blk", None), P("blk", None)),
        out_specs=(P("blk", None), P("blk", None), P("blk", None)),
        check_vma=False,
    )
```

```python
import functools

import jax
import jax.numpy as jnp
from jax import lax
from jax.experimental import pallas as pl
from jax.experimental.pallas import tpu as pltpu
from jax.sharding import PartitionSpec as P

momentum = 0.5
step_scale = 8.0
third_stride = 3
MESH = pl.DeviceIdType.MESH
NT = (((1,), (1,)), ((), ()))


def halves(x):
    high = x.astype(jnp.bfloat16)
    low = (x - high.astype(jnp.float32)).astype(jnp.bfloat16)
    return high, low


def dot(a, b):
    return jnp.dot(a, b, preferred_element_type=jnp.float32)


def kernel(
    count, strata, rates,
    blocks, first, second, third,
    first_out, second_out, third_out,
    target, rows_a, vel_a, grad_a, grad_c,
    recv_b, recv_c, send_b, send_c, past_b, past_c,
    keep_out_b, keep_out_c, keep_in_b, keep_in_c, last_b, last_c,
    cat_k, cat_r, pair_h, pair_l, miss, turn_h, turn_l,
    t_sem, b_sem, c_sem, pb_sem, pc_sem, kb_sem, kc_sem, lb_sem, lc_sem,
):
    rate_a, rate_b, rate_c = rates
    me = lax.axis_index("blk")
    i_rows = first.shape[0]
    j_rows, rank = second.shape
    k_rows = third.shape[0]
    wide = 2 * k_rows

    def other(by):
        return lax.rem(me + (by % count), count)

    def to(src, dst, sem, by):
        return pltpu.make_async_remote_copy(
            src_ref=src, dst_ref=dst, send_sem=sem.at[0], recv_sem=sem.at[1],
            device_id=(other(by),), device_id_type=MESH,
        )

    hops = set()
    for reach in (1, strata - 2, strata - 1):
        hops |= {reach, -reach, third_stride * reach, -third_stride * reach}
    hops = sorted(hops)
    barrier = pltpu.get_barrier_semaphore()
    for by in hops:
        pl.semaphore_signal(barrier, inc=1, device_id=(other(by),), device_id_type=MESH)
    loads = [
        pltpu.make_async_copy(blocks.at[s], target.at[s], t_sem.at[s]) for s in range(strata)
    ]
    for load in loads:
        load.start()

    rows_a[...] = first[...]
    sent = []
    for s in range(strata):
        if s == 0:
            b_ref, c_ref = second, third
        else:
            b_ref, c_ref = recv_b.at[s - 1], recv_c.at[s - 1]
            moved_c.wait_recv()
            moved_b.wait_recv()
        if s + 2 < strata:
            past = (
                to(c_ref, past_c.at[s], pc_sem.at[s], -third_stride),
                to(b_ref, past_b.at[s], pb_sem.at[s], -1),
            )
            if s > 0 and not False:
                for copy in past:
                    copy.start()
            sent.extend(past)
        b_high, b_low = halves(b_ref[...])
        cat_k[...] = jnp.concatenate([b_high, b_high, b_low], axis=1)
        cat_r[...] = jnp.concatenate([b_high, b_high, b_low], axis=0)
        loads[s].wait()

        def model(p, _):
            c = c_ref[...]
            a0 = rows_a[pl.ds(2 * p, 1), :]
            a1 = rows_a[pl.ds(2 * p + 1, 1), :]
            high, low = halves(jnp.concatenate([c * a0, c * a1], axis=0))
            at = pl.multiple_of(p * wide, wide)
            pair_h[pl.ds(at, wide), :] = high
            pair_l[pl.ds(at, wide), :] = low
            made = lax.dot_general(
                cat_k[...], jnp.concatenate([high, low, high], axis=1), NT,
                preferred_element_type=jnp.float32,
            )
            want = jnp.concatenate([target[s, 2 * p], target[s, 2 * p + 1]], axis=1)
            high, low = halves(made - want)
            miss[pl.ds(0, j_rows), pl.ds(at, wide)] = high
            miss[pl.ds(j_rows, j_rows), pl.ds(at, wide)] = low
            turn_h[pl.ds(at, wide), :] = high.T
            turn_l[pl.ds(at, wide), :] = low.T
            return 0

        lax.fori_loop(0, i_rows // 2, model, 0, unroll=8)

        both = dot(miss[...], pair_h[...])
        grad = both[:j_rows] + both[j_rows:] + dot(miss[pl.ds(0, j_rows), :], pair_l[...])
        step_b = rate_b * grad
        if s == 0:
            pl.semaphore_wait(barrier, len(hops))
        if s + 1 == strata:
            send_b[s] = step_b
            moved_b = to(send_b.at[s], last_b, lb_sem, strata - 1)
            moved_b.start()
        else:
            now = b_ref[...]
            if s > 0:
                old_b.wait_recv()
                keep = momentum * (now - past_b[s - 1])
                now = now + keep
                vel = keep - step_b
            else:
                vel = -step_b
            now = now - step_b
            send_b[s] = now
            moved_b = to(send_b.at[s], recv_b.at[s], b_sem.at[s], -1)
            moved_b.start()
            if s + 2 == strata:
                keep_out_b[...] = now + momentum * vel
        sent.append(moved_b)

        grad_c[...] = jnp.zeros_like(grad_c)

        def spread(p, _):
            at = pl.multiple_of(p * wide, wide)
            high = turn_h[pl.ds(at, wide), :]
            low = turn_l[pl.ds(at, wide), :]
            d = dot(jnp.concatenate([high, low, high], axis=1), cat_r[...])
            c = c_ref[...]
            a0 = rows_a[pl.ds(2 * p, 1), :]
            a1 = rows_a[pl.ds(2 * p + 1, 1), :]
            grad_c[...] += a0 * d[:k_rows] + a1 * d[k_rows:]
            grad_a[pl.ds(2 * p, 1), :] = jnp.sum(c * d[:k_rows], axis=0, keepdims=True)
            grad_a[pl.ds(2 * p + 1, 1), :] = jnp.sum(c * d[k_rows:], axis=0, keepdims=True)
            return 0

        lax.fori_loop(0, i_rows // 2, spread, 0, unroll=8)

        step_c = rate_c * grad_c[...]
        if s + 1 == strata:
            send_c[s] = step_c
            moved_c = to(send_c.at[s], last_c, lc_sem, third_stride * (strata - 1))
            moved_c.start()
        else:
            now = c_ref[...]
            if s > 0:
                old_c.wait_recv()
                keep = momentum * (now - past_c[s - 1])
                now = now + keep
                vel = keep - step_c
            else:
                vel = -step_c
            now = now - step_c
            send_c[s] = now
            moved_c = to(send_c.at[s], recv_c.at[s], c_sem.at[s], -third_stride)
            moved_c.start()
            if s + 2 == strata:
                keep_out_c[...] = now + momentum * vel
                kept_b = to(keep_out_b, keep_in_b, kb_sem, strata - 2)
                kept_c = to(keep_out_c, keep_in_c, kc_sem, third_stride * (strata - 2))
                kept_b.start()
                kept_c.start()
                sent.extend([kept_b, kept_c])
        sent.append(moved_c)
        if s + 2 < strata:
            if s == 0 or False:
                for copy in past:
                    copy.start()
            old_c, old_b = past

        step_a = rate_a * grad_a[...]
        if s == 0:
            rows_a[...] = rows_a[...] - step_a
            vel_a[...] = -step_a
        else:
            keep = momentum * vel_a[...]
            rows_a[...] = (rows_a[...] + keep) - step_a
            vel_a[...] = keep - step_a

    first_out[...] = rows_a[...]
    kept_b.wait_recv()
    moved_b.wait_recv()
    second_out[...] = keep_in_b[...] - last_b[...]
    kept_c.wait_recv()
    moved_c.wait_recv()
    third_out[...] = keep_in_c[...] - last_c[...]
    for copy in sent:
        copy.wait_send()


def shards(count, blocks, first, second, third):
    strata = blocks.shape[0]
    i_rows, rank = first.shape
    j_rows = second.shape[0]
    k_rows = third.shape[0]
    rates = (
        step_scale / (j_rows * k_rows),
        step_scale / (i_rows * k_rows),
        step_scale / (i_rows * j_rows),
    )
    f32, bf16 = jnp.float32, jnp.bfloat16
    a, b, c = (i_rows, rank), (j_rows, rank), (k_rows, rank)
    pairs = i_rows * k_rows
    vmem = pl.BlockSpec(memory_space=pltpu.VMEM)
    dma = pltpu.SemaphoreType.DMA
    return pl.pallas_call(
        functools.partial(kernel, count, strata, rates),
        out_shape=[jax.ShapeDtypeStruct(x, f32) for x in (a, b, c)],
        in_specs=[pl.BlockSpec(memory_space=pl.ANY), vmem, vmem, vmem],
        out_specs=[vmem, vmem, vmem],
        scratch_shapes=[
            pltpu.VMEM(blocks.shape, f32),
            pltpu.VMEM(a, f32), pltpu.VMEM(a, f32), pltpu.VMEM(a, f32), pltpu.VMEM(c, f32),
            pltpu.VMEM((strata - 1,) + b, f32), pltpu.VMEM((strata - 1,) + c, f32),
            pltpu.VMEM((strata,) + b, f32), pltpu.VMEM((strata,) + c, f32),
            pltpu.VMEM((strata - 2,) + b, f32), pltpu.VMEM((strata - 2,) + c, f32),
            pltpu.VMEM(b, f32), pltpu.VMEM(c, f32),
            pltpu.VMEM(b, f32), pltpu.VMEM(c, f32),
            pltpu.VMEM(b, f32), pltpu.VMEM(c, f32),
            pltpu.VMEM((j_rows, 3 * rank), bf16), pltpu.VMEM((3 * j_rows, rank), bf16),
            pltpu.VMEM((pairs, rank), bf16), pltpu.VMEM((pairs, rank), bf16),
            pltpu.VMEM((2 * j_rows, pairs), bf16),
            pltpu.VMEM((pairs, j_rows), bf16), pltpu.VMEM((pairs, j_rows), bf16),
            dma((strata,)),
            dma((strata - 1, 2)), dma((strata - 1, 2)),
            dma((strata - 2, 2)), dma((strata - 2, 2)),
            dma((2,)), dma((2,)), dma((2,)), dma((2,)),
        ],
        compiler_params=pltpu.CompilerParams(
            collective_id=0, has_side_effects=True, vmem_limit_bytes=48 * 1024 * 1024,
        ),
        cost_estimate=pl.CostEstimate(
            flops=strata * 18 * pairs * j_rows * rank,
            bytes_accessed=4 * strata * i_rows * j_rows * k_rows, transcendentals=0,
        ),
    )(blocks, first, second, third)


def solution(mesh):
    return jax.shard_map(
        functools.partial(shards, mesh.shape["blk"]),
        mesh=mesh,
        in_specs=(P(None, "blk", None, None), P("blk", None), P("blk", None), P("blk", None)),
        out_specs=(P("blk", None), P("blk", None), P("blk", None)),
        check_vma=False,
    )
```
